32 devices in a mesh: hours: 2 (over x), row: 8 (over z, y), col: 2 (over core).
Axes of the slice: x: 2, y: 2, z: 4, core: 2. Of those that a mesh axis runs over, the one named last changes fastest.
Arguments:
- spectra: bfloat16 [24, 2, 64, 4096], P('hours', None, 'row', 'col'), parts along dimension 0, may hold values from -6 to 6
- masks: int32 [24, 64], P('hours', 'row'), parts along dimension 0, may hold values 0 or 1
Outputs:
- correlations: float32 [128, 2, 32, 128], P(('hours', 'row'), 'col'), parts along dimension 0
The draws below stay inside these ranges and needn't reach their ends.
There are 2 independent parts, one for each index of `hours`. The reference program is written for one: setup_inputs(seed, part) draws one part's arguments, and reference() takes and returns one part's arrays. A program takes and returns all parts, laid end to end along the dimension named above; each array names one. Nothing has to cross between parts.
All inputs are finite; a program needn't handle non-finite values. No bound on the sum of `masks` on one device may be relied on, other than what follows from the above.
Results may differ from the reference program's by a relative error of at most 0.0054.
Values may be sent and summed in bfloat16 or wider, within the bound.
A program may use at most 128 MiB of HBM per device.

```python
import math
import jax
import jax.numpy as jnp
from jax import lax

CH_DEV = 8
WINDOWS = 12
F = 4096
SMOOTH = 32
LAGS = 128
NCH = 64
GROUPS = 2
PART_CH = 4


def with_ends(entries, own_key, least, largest):
    index_at = [jax.random.randint(jax.random.fold_in(own_key, axis), (), 0, length) for axis, length in enumerate(entries.shape)]
    main_axis = entries.shape.index(max(entries.shape))
    beside = index_at[:main_axis] + [(index_at[main_axis] + 1) % entries.shape[main_axis]] + index_at[main_axis + 1:]
    return entries.at[tuple(index_at)].set(least).at[tuple(beside)].set(largest)


def shard_levels(stream_key, dims, pieces, smallest, largest):
    def one(axis_at, blocks):
        draws = jax.random.uniform(jax.random.fold_in(jax.random.fold_in(stream_key, 6), axis_at), (blocks,), jnp.float32, smallest / len(pieces), largest / len(pieces))
        return jnp.repeat(jnp.exp(draws), dims[axis_at] // blocks).reshape((-1,) + (1,) * (len(dims) - axis_at - 1))

    gain = one(*pieces[0])
    for cut in pieces[1:]:
        gain = gain * one(*cut)
    return gain


def gaussian(stream_key, shape, width, most, pieces=(), kind=jnp.bfloat16):
    values = width * jax.random.normal(stream_key, shape, jnp.float32)
    if pieces:
        values = values * shard_levels(stream_key, shape, pieces, -0.22, 0.18)
    return jnp.clip(values, -most, most).astype(kind)


def setup_inputs(seed: int = 0, part: int = 0) -> dict:
    key_list = jax.random.split(jax.random.key(seed), 3)
    own_keys = jax.random.split(jax.random.fold_in(key_list[2], part), 3)
    return {
        "spectra": gaussian(own_keys[0], (WINDOWS, 2, NCH, F), 1.0, 6.0, ((2, 8), (3, 2))),
        "masks": with_ends((jax.random.randint(own_keys[1], (WINDOWS, NCH), 0, 4) < 3).astype(jnp.int32), jax.random.fold_in(own_keys[1], 1), 0, 1),
    }


EPSILON = 1e-05

def cosine_table(first, count):
    freqs = first + jnp.arange(count, dtype=jnp.int32)
    shifts = jnp.arange(1, LAGS + 1, dtype=jnp.int32)
    phase = freqs[:, None] * shifts[None, :] % (2 * F)
    angle = jnp.pi * phase.astype(jnp.float32) / F
    factor = 1.0 / math.sqrt(F)
    return jnp.concatenate([jnp.cos(angle) * factor, -jnp.sin(angle) * factor], axis=0).astype(jnp.bfloat16)

def whiten(values, padded, live):
    total = lax.reduce_window(padded, jnp.array(0, padded.dtype), lax.add, (1, 1, 2 * SMOOTH + 1), (1, 1, 1), 'VALID')
    amplitude = total / (2 * SMOOTH + 1) + EPSILON
    return (values / amplitude[:, None] * live[:, None, :, None]).astype(jnp.bfloat16)

def correlate(own, own_live, other, other_live, table):
    form = 'wif,wjf->ijf'
    high = lax.Precision.HIGHEST
    real = jnp.einsum(form, own[:, 0], other[:, 0], precision=high) + jnp.einsum(form, own[:, 1], other[:, 1], precision=high)
    imag = jnp.einsum(form, own[:, 1], other[:, 0], precision=high) - jnp.einsum(form, own[:, 0], other[:, 1], precision=high)
    count = jnp.maximum(jnp.einsum('wi,wj->ij', own_live, other_live, precision=high), 1.0)
    stacked = (jnp.stack([real, imag], axis=2) / count[:, :, None, None]).astype(jnp.bfloat16)
    rows = stacked.reshape(stacked.shape[0] * stacked.shape[1], -1)
    result = jnp.dot(rows, table, preferred_element_type=jnp.float32)
    return result.reshape(stacked.shape[0], stacked.shape[1], -1)

def reference(spectra, masks):
    values = spectra.astype(jnp.float32)
    magnitude = jnp.sqrt(values[:, 0] * values[:, 0] + values[:, 1] * values[:, 1])
    padded = jnp.pad(magnitude, ((0, 0), (0, 0), (SMOOTH, SMOOTH)))
    live = masks.astype(jnp.float32)
    whitened = whiten(values, padded, live)
    table = cosine_table(0, F)
    widened = whitened.astype(jnp.float32)
    blocks = NCH // CH_DEV

    def one_block(block):
        own = lax.dynamic_slice_in_dim(widened, block * CH_DEV, CH_DEV, 2)
        own_live = lax.dynamic_slice_in_dim(live, block * CH_DEV, CH_DEV, 1)
        return correlate(own, own_live, widened, live, table)
    result = lax.map(one_block, jnp.arange(blocks, dtype=jnp.int32))
    result = result.reshape(NCH, blocks, GROUPS, PART_CH, LAGS)
    result = jnp.transpose(result, (0, 2, 1, 3, 4))
    return result.reshape(NCH, GROUPS, NCH // GROUPS, LAGS)
```

```python
import functools
import math

import jax
import jax.numpy as jnp
from jax import lax
from jax.experimental import pallas as pl
from jax.experimental.pallas import tpu as pltpu
from jax.sharding import PartitionSpec as P

F = 4096
SMOOTH = 32
LAGS = 128
EPSILON = 1e-05
LANES = 128
GROUP_SPLIT = 3
MESH = pl.DeviceIdType.MESH


def shifted(cells, by):
    return pltpu.roll(cells, (-by) % cells.shape[1], 1)


def kernel(
    rows, x_ref, m_ref, out_ref,
    mag, halo_out, halo_in, marks, live, sbuf, rbuf, re, im, su, di, table, part, mate, got,
    halo_sem, mark_send, mark_recv, a2a_send, a2a_recv, own_sem, mate_send, mate_recv, row_send, row_recv,
):
    windows, _, ch, half = x_ref.shape
    bins = half // rows
    hours, me, col = lax.axis_index("hours"), lax.axis_index("row"), lax.axis_index("col")
    other = 1 - col
    step_w = windows // GROUP_SPLIT

    def peer(k):
        return lax.rem(me + k, rows)

    def at_row(r):
        return (hours, r, col)

    at_mate = (hours, me, other)

    barrier = pltpu.get_barrier_semaphore()
    for k in range(1, rows):
        pl.semaphore_signal(barrier, inc=1, device_id=at_row(peer(k)), device_id_type=MESH)
    pl.semaphore_signal(barrier, inc=1, device_id=at_mate, device_id_type=MESH)

    def magnitude(a, b):
        return jnp.sqrt(a * a + b * b)

    def edges(w, _):
        a = x_ref[w, 0, :, half - LANES:].astype(jnp.float32)
        b = x_ref[w, 1, :, half - LANES:].astype(jnp.float32)
        c = x_ref[w, 0, :, :LANES].astype(jnp.float32)
        d = x_ref[w, 1, :, :LANES].astype(jnp.float32)
        first = col == 0
        halo_out[w] = magnitude(jnp.where(first, a, c), jnp.where(first, b, d))
        return 0

    lax.fori_loop(0, windows, edges, 0)

    lane = lax.broadcasted_iota(jnp.int32, (ch, LANES), 1)
    diag = lax.broadcasted_iota(jnp.int32, (ch, ch), 0) == lax.broadcasted_iota(jnp.int32, (ch, ch), 1)
    packed = jnp.zeros((ch, LANES), jnp.float32)
    for w in range(windows):
        row = m_ref[w:w + 1, :].astype(jnp.float32)
        column = jnp.sum(jnp.where(diag, row, 0.0), axis=1, keepdims=True)
        wide = jnp.broadcast_to(column, (ch, LANES))
        live[w] = wide
        packed = jnp.where(lane == w, wide, packed)
    marks[me] = packed

    pl.semaphore_wait(barrier, rows)

    halo = pltpu.make_async_remote_copy(
        src_ref=halo_out, dst_ref=halo_in, send_sem=halo_sem.at[0], recv_sem=halo_sem.at[1],
        device_id=at_mate, device_id_type=MESH,
    )
    halo.start()

    def mark_copy(k):
        return pltpu.make_async_remote_copy(
            src_ref=marks.at[me], dst_ref=marks.at[me], send_sem=mark_send.at[k], recv_sem=mark_recv.at[k],
            device_id=at_row(peer(k)), device_id_type=MESH,
        )

    for k in range(1, rows):
        mark_copy(k).start()

    def fill(w, _):
        a = x_ref[w, 0].astype(jnp.float32)
        b = x_ref[w, 1].astype(jnp.float32)
        mag[w, :, LANES:LANES + half] = magnitude(a, b)
        return 0

    lax.fori_loop(0, windows, fill, 0)
    halo.wait()

    def whiten(w, _):
        edge = halo_in[w]
        zero = jnp.zeros_like(edge)
        cells = jnp.concatenate(
            [jnp.where(col == 0, zero, edge), mag[w, :, LANES:LANES + half], jnp.where(col == 0, edge, zero)], axis=1
        )
        total = cells
        for by in (1, 2, 4, 8, 16):
            total = total + shifted(total, by)
        total = total + shifted(total, -SMOOTH) + shifted(cells, SMOOTH)
        total = total[:, LANES:LANES + half]
        amplitude = total / (2 * SMOOTH + 1) + EPSILON
        scale = live[w][:, :1] / amplitude
        both = jnp.concatenate(
            [x_ref[w, 0].astype(jnp.float32) * scale, x_ref[w, 1].astype(jnp.float32) * scale], axis=0
        ).astype(jnp.bfloat16)
        for r in range(rows):
            sbuf[r, w] = both[:, r * bins:(r + 1) * bins]
        return 0

    def share(g, k):
        span = pl.ds(g * step_w, step_w)
        return pltpu.make_async_remote_copy(
            src_ref=sbuf.at[peer(k), span], dst_ref=rbuf.at[me, span],
            send_sem=a2a_send.at[g, k], recv_sem=a2a_recv.at[g, k],
            device_id=at_row(peer(k)), device_id_type=MESH,
        )

    for g in range(GROUP_SPLIT):
        lax.fori_loop(g * step_w, (g + 1) * step_w, whiten, 0)
        for k in range(1, rows):
            share(g, k).start()

    own = pltpu.make_async_copy(sbuf.at[me], rbuf.at[me], own_sem)
    own.start()

    first = col * half + me * bins
    freq = first + lax.broadcasted_iota(jnp.int32, (bins, LAGS), 0)
    lag = 1 + lax.broadcasted_iota(jnp.int32, (bins, LAGS), 1)
    phase = freq * lag
    for p in range(2):
        turn = jnp.bitwise_and(phase + p * (F // 2), 2 * F - 1)
        wave = jnp.cos(turn.astype(jnp.float32) * (math.pi / F)) * (1.0 / math.sqrt(F))
        table[p * bins:(p + 1) * bins, :LAGS] = wave.astype(jnp.bfloat16)
        table[p * bins:(p + 1) * bins, LAGS:] = (wave if p == 0 else -wave).astype(jnp.bfloat16)

    own.wait()

    def widen(source):
        def one(w, _):
            both = rbuf[source, w].astype(jnp.float32)
            a, b = both[:ch], both[ch:]
            re[source, w] = a
            im[source, w] = b
            su[source, w] = a + b
            di[source, w] = a - b
            return 0

        lax.fori_loop(0, windows, one, 0)

    widen(me)
    for k in range(1, rows):
        mark_copy(k).wait_send()
        for g in range(GROUP_SPLIT):
            share(g, k).wait_send()

    def arrived(k, _):
        source = lax.rem(me + rows - k, rows)
        pltpu.make_async_remote_copy(
            src_ref=marks.at[source], dst_ref=marks.at[source], send_sem=mark_send.at[k], recv_sem=mark_recv.at[k],
            device_id=at_row(peer(k)), device_id_type=MESH,
        ).wait_recv()
        for g in range(GROUP_SPLIT):
            span = pl.ds(g * step_w, step_w)
            pltpu.make_async_remote_copy(
                src_ref=sbuf.at[source, span], dst_ref=rbuf.at[source, span],
                send_sem=a2a_send.at[g, k], recv_sem=a2a_recv.at[g, k],
                device_id=at_row(peer(k)), device_id_type=MESH,
            ).wait_recv()
        widen(source)
        return 0

    lax.fori_loop(1, rows, arrived, 0)

    quarter = ch // 2

    def pair(block_i, block_j):
        right = [(re[block_j, w], im[block_j, w], di[block_j, w]) for w in range(windows)]
        real, imag = [], []
        marks_j = marks[block_j]
        for i in range(ch):
            k1 = k2 = k3 = None
            for w in range(windows):
                c, d, e = right[w]
                a = re[block_i, w, i:i + 1, :]
                b = im[block_i, w, i:i + 1, :]
                s = su[block_i, w, i:i + 1, :]
                k1 = a * c if k1 is None else k1 + a * c
                k2 = b * d if k2 is None else k2 + b * d
                k3 = s * e if k3 is None else k3 + s * e
            count = jnp.sum(marks[block_i, i:i + 1, :] * marks_j, axis=1, keepdims=True)
            scale = 1.0 / jnp.maximum(count, 1.0)
            real.append((k1 + k2) * scale)
            imag.append((k3 - k1 + k2) * scale)
        left = jnp.concatenate(
            [jnp.concatenate(real, axis=0), jnp.concatenate(imag, axis=0)], axis=1
        ).astype(jnp.bfloat16)
        result = jnp.dot(left, table[...], preferred_element_type=jnp.float32)
        for i in range(ch):
            tile = result[i * ch:(i + 1) * ch]
            for h in range(2):
                part[h, block_i, i, block_j] = tile[h * quarter:(h + 1) * quarter, :LAGS]
            mirror = tile[:, LAGS:]
            for j in range(ch):
                part[i // quarter, block_j, j, block_i, i % quarter:i % quarter + 1, :] = mirror[j:j + 1, :]

    def owner(n):
        return lax.rem(me + 1 + n, rows)

    def to_mate(n):
        r = owner(n)
        return pltpu.make_async_remote_copy(
            src_ref=part.at[other, r], dst_ref=mate.at[r], send_sem=mate_send.at[n], recv_sem=mate_recv.at[n],
            device_id=at_mate, device_id_type=MESH,
        )

    def to_row(n):
        r = owner(n)
        return pltpu.make_async_remote_copy(
            src_ref=part.at[col, r], dst_ref=got.at[me], send_sem=row_send.at[n], recv_sem=row_recv.at[n],
            device_id=at_row(r), device_id_type=MESH,
        )

    def fold(n):
        to_mate(n).wait_recv()
        r = owner(n)
        for i in range(ch):
            part[col, r, i] = part[col, r, i] + mate[r, i]

    def sweep(n, _):
        def inner(m, _):
            pair(owner(n), owner(m))
            return 0

        lax.fori_loop(n, rows, inner, 0)
        to_mate(n).start()

        @pl.when(n > 0)
        def _():
            fold(n - 1)
            to_row(n - 1).start()

        return 0

    lax.fori_loop(0, rows, sweep, 0)
    fold(rows - 1)

    for i in range(ch):
        out_ref[i, 0] = part[col, me, i].reshape(rows * quarter, LAGS)

    def collect(n, _):
        source = lax.rem(me + rows + rows - 1 - n, rows)
        pltpu.make_async_remote_copy(
            src_ref=part.at[col, source], dst_ref=got.at[source], send_sem=row_send.at[n], recv_sem=row_recv.at[n],
            device_id=at_row(owner(n)), device_id_type=MESH,
        ).wait_recv()
        for i in range(ch):
            out_ref[i, 0] = out_ref[i, 0] + got[source, i].reshape(rows * quarter, LAGS)
        return 0

    lax.fori_loop(0, rows - 1, collect, 0)
    for n in range(rows):
        to_mate(n).wait_send()
        if n < rows - 1:
            to_row(n).wait_send()


def fused(spectra, masks):
    windows, _, ch, half = spectra.shape
    rows = lax.axis_size("row")
    bins = half // rows
    quarter = ch // 2
    f32, bf16 = jnp.float32, jnp.bfloat16
    dma = pltpu.SemaphoreType.DMA
    return pl.pallas_call(
        functools.partial(kernel, rows),
        out_shape=jax.ShapeDtypeStruct((ch, 1, rows * quarter, LAGS), f32),
        in_specs=[pl.BlockSpec(memory_space=pltpu.VMEM)] * 2,
        out_specs=pl.BlockSpec(memory_space=pltpu.VMEM),
        scratch_shapes=[
            pltpu.VMEM((windows, ch, half + 2 * LANES), f32),
            pltpu.VMEM((windows, ch, LANES), f32),
            pltpu.VMEM((windows, ch, LANES), f32),
            pltpu.VMEM((rows, ch, LANES), f32),
            pltpu.VMEM((windows, ch, LANES), f32),
            pltpu.VMEM((rows, windows, 2 * ch, bins), bf16),
            pltpu.VMEM((rows, windows, 2 * ch, bins), bf16),
            pltpu.VMEM((rows, windows, ch, bins), f32),
            pltpu.VMEM((rows, windows, ch, bins), f32),
            pltpu.VMEM((rows, windows, ch, bins), f32),
            pltpu.VMEM((rows, windows, ch, bins), f32),
            pltpu.VMEM((2 * bins, 2 * LAGS), bf16),
            pltpu.VMEM((2, rows, ch, rows, quarter, LAGS), f32),
            pltpu.VMEM((rows, ch, rows, quarter, LAGS), f32),
            pltpu.VMEM((rows, ch, rows, quarter, LAGS), f32),
            dma((2,)),
            dma((rows,)),
            dma((rows,)),
            dma((GROUP_SPLIT, rows)),
            dma((GROUP_SPLIT, rows)),
            dma,
            dma((rows,)),
            dma((rows,)),
            dma((rows,)),
            dma((rows,)),
        ],
        compiler_params=pltpu.CompilerParams(
            collective_id=0, has_side_effects=True, vmem_limit_bytes=48 * 1024 * 1024
        ),
    )(spectra, masks)


def with_halo(cells, width):
    head = cells[..., :width]
    tail = cells[..., cells.shape[-1] - width:]
    return jnp.concatenate(
        [lax.ppermute(tail, "col", [(0, 1)]), cells, lax.ppermute(head, "col", [(1, 0)])], axis=-1
    )


def cosine_table(first, count):
    freqs = first + jnp.arange(count, dtype=jnp.int32)
    shifts = jnp.arange(1, LAGS + 1, dtype=jnp.int32)
    phase = freqs[:, None] * shifts[None, :] % (2 * F)
    angle = jnp.pi * phase.astype(jnp.float32) / F
    factor = 1.0 / math.sqrt(F)
    return jnp.concatenate([jnp.cos(angle) * factor, -jnp.sin(angle) * factor], axis=0).astype(jnp.bfloat16)


def correlate(own, own_live, far, far_live, table):
    a, b = own[:, 0].astype(jnp.float32), own[:, 1].astype(jnp.float32)
    c, d = far[:, 0].astype(jnp.float32), far[:, 1].astype(jnp.float32)
    shape = (own.shape[2], far.shape[2], own.shape[3])
    real = jnp.zeros(shape, jnp.float32)
    imag = jnp.zeros(shape, jnp.float32)
    for w in range(own.shape[0]):
        real = real + (a[w, :, None] * c[w, None] + b[w, :, None] * d[w, None])
        imag = imag + (b[w, :, None] * c[w, None] - a[w, :, None] * d[w, None])
    count = jnp.maximum(jnp.dot(own_live.T, far_live, preferred_element_type=jnp.float32), 1.0)
    stacked = (jnp.stack([real, imag], axis=2) / count[:, :, None, None]).astype(jnp.bfloat16)
    lines = stacked.reshape(shape[0] * shape[1], -1)
    return jnp.dot(lines, table, preferred_element_type=jnp.float32).reshape(shape[0], shape[1], LAGS)


def ring(spectra, masks):
    ch, half = spectra.shape[2], spectra.shape[3]
    rows = lax.axis_size("row")
    me, col = lax.axis_index("row"), lax.axis_index("col")
    quarter = ch // 2
    live = masks.astype(jnp.float32)
    values = spectra.astype(jnp.float32)
    padded = with_halo(jnp.sqrt(values[:, 0] * values[:, 0] + values[:, 1] * values[:, 1]), SMOOTH)
    total = padded
    for by in (1, 2, 4, 8, 16, 32):
        total = total[..., :-by] + total[..., by:]
    total = total[..., :half] + padded[..., 2 * SMOOTH:]
    amplitude = total / (2 * SMOOTH + 1) + EPSILON
    whitened = (values / amplitude[:, None] * live[:, None, :, None]).astype(jnp.bfloat16)
    table = cosine_table(col * half, half)
    onward = [(r, (r + 1) % rows) for r in range(rows)]

    def step(n, carry):
        result, far, marks = carry
        block = correlate(whitened, live, far, marks.astype(jnp.float32), table)
        block = block.reshape(ch, 2, quarter, LAGS)
        source = lax.rem(me + rows - n, rows)
        result = lax.dynamic_update_slice(result, block, (0, 0, source * quarter, 0))
        return result, lax.ppermute(far, "row", onward), lax.ppermute(marks, "row", onward)

    empty = jnp.zeros((ch, 2, rows * quarter, LAGS), jnp.float32)
    result, _, _ = lax.fori_loop(0, rows, step, (empty, whitened, live.astype(jnp.bfloat16)))
    mine = lax.dynamic_slice_in_dim(result, col, 1, 1)
    other = lax.dynamic_slice_in_dim(result, 1 - col, 1, 1)
    return mine + lax.ppermute(other, "col", [(0, 1), (1, 0)])


def per_device(spectra, masks):
    windows, _, ch, half = spectra.shape
    rows = lax.axis_size("row")
    bins = half // rows
    fits = rows <= 8 and ch == 8 and bins % LANES == 0 and windows % GROUP_SPLIT == 0 and windows <= LANES
    return fused(spectra, masks) if fits else ring(spectra, masks)


def solution(mesh):
    return jax.shard_map(
        per_device,
        mesh=mesh,
        in_specs=(P("hours", None, "row", "col"), P("hours", "row")),
        out_specs=P(("hours", "row"), "col", None, None),
        check_vma=False,
    )
```

```python
import functools
import math

import jax
import jax.numpy as jnp
from jax import lax
from jax.experimental import pallas as pl
from jax.experimental.pallas import tpu as pltpu
from jax.sharding import PartitionSpec as P

F = 4096
SMOOTH = 32
LAGS = 128
EPSILON = 1e-05
LANES = 128
GROUP_SPLIT = 3
MESH = pl.DeviceIdType.MESH


def shifted(cells, by):
    return pltpu.roll(cells, (-by) % cells.shape[1], 1)


def kernel(
    rows, x_ref, m_ref, out_ref,
    mag, halo_out, halo_in, marks, live, sbuf, rbuf, re, im, su, di, table, stash, part, mate, near, got,
    halo_sem, mark_send, mark_recv, a2a_send, a2a_recv, own_sem, mate_send, mate_recv, near_send, near_recv, row_send, row_recv,
):
    windows, _, ch, half = x_ref.shape
    bins = half // rows
    part_bins = bins // 2
    pairs = rows // 2
    hours, me, col = lax.axis_index("hours"), lax.axis_index("row"), lax.axis_index("col")
    other = 1 - col
    step_w = windows // GROUP_SPLIT

    def peer(k):
        return lax.rem(me + k, rows)

    def at_row(r):
        return (hours, r, col)

    at_mate = (hours, me, other)

    barrier = pltpu.get_barrier_semaphore()
    for k in range(1, rows):
        pl.semaphore_signal(barrier, inc=1, device_id=at_row(peer(k)), device_id_type=MESH)
    pl.semaphore_signal(barrier, inc=1, device_id=at_mate, device_id_type=MESH)

    def magnitude(a, b):
        return jnp.sqrt(a * a + b * b)

    def edges(w, _):
        a = x_ref[w, 0, :, half - LANES:].astype(jnp.float32)
        b = x_ref[w, 1, :, half - LANES:].astype(jnp.float32)
        c = x_ref[w, 0, :, :LANES].astype(jnp.float32)
        d = x_ref[w, 1, :, :LANES].astype(jnp.float32)
        first = col == 0
        halo_out[w] = magnitude(jnp.where(first, a, c), jnp.where(first, b, d))
        return 0

    lax.fori_loop(0, windows, edges, 0)

    lane = lax.broadcasted_iota(jnp.int32, (ch, LANES), 1)
    diag = lax.broadcasted_iota(jnp.int32, (ch, ch), 0) == lax.broadcasted_iota(jnp.int32, (ch, ch), 1)
    packed = jnp.zeros((ch, LANES), jnp.float32)
    for w in range(windows):
        row = m_ref[w:w + 1, :].astype(jnp.float32)
        column = jnp.sum(jnp.where(diag, row, 0.0), axis=1, keepdims=True)
        wide = jnp.broadcast_to(column, (ch, LANES))
        live[w] = wide
        packed = jnp.where(lane == w, wide, packed)
    marks[me] = packed

    pl.semaphore_wait(barrier, rows)

    halo = pltpu.make_async_remote_copy(
        src_ref=halo_out, dst_ref=halo_in, send_sem=halo_sem.at[0], recv_sem=halo_sem.at[1],
        device_id=at_mate, device_id_type=MESH,
    )
    halo.start()

    def mark_copy(k):
        return pltpu.make_async_remote_copy(
            src_ref=marks.at[me], dst_ref=marks.at[me], send_sem=mark_send.at[k], recv_sem=mark_recv.at[k],
            device_id=at_row(peer(k)), device_id_type=MESH,
        )

    for k in range(1, rows):
        mark_copy(k).start()

    def fill(w, _):
        a = x_ref[w, 0].astype(jnp.float32)
        b = x_ref[w, 1].astype(jnp.float32)
        mag[w, :, LANES:LANES + half] = magnitude(a, b)
        return 0

    lax.fori_loop(0, windows, fill, 0)
    halo.wait()

    def whiten(w, _):
        edge = halo_in[w]
        zero = jnp.zeros_like(edge)
        cells = jnp.concatenate(
            [jnp.where(col == 0, zero, edge), mag[w, :, LANES:LANES + half], jnp.where(col == 0, edge, zero)], axis=1
        )
        total = cells
        for by in (1, 2, 4, 8, 16):
            total = total + shifted(total, by)
        total = total + shifted(total, -SMOOTH) + shifted(cells, SMOOTH)
        total = total[:, LANES:LANES + half]
        amplitude = total / (2 * SMOOTH + 1) + EPSILON
        scale = live[w][:, :1] / amplitude
        both = jnp.concatenate(
            [x_ref[w, 0].astype(jnp.float32) * scale, x_ref[w, 1].astype(jnp.float32) * scale], axis=0
        ).astype(jnp.bfloat16)
        for r in range(rows):
            for t in range(2):
                start = r * bins + t * part_bins
                sbuf[r, t, w] = both[:, start:start + part_bins]
        return 0

    def share(g, k):
        if g < GROUP_SPLIT:
            span = pl.ds(g * step_w, step_w)
            source, target = sbuf.at[peer(k), 0, span], rbuf.at[me, 0, span]
        else:
            source, target = sbuf.at[peer(k), 1], rbuf.at[me, 1]
        return pltpu.make_async_remote_copy(
            src_ref=source, dst_ref=target, send_sem=a2a_send.at[g, k], recv_sem=a2a_recv.at[g, k],
            device_id=at_row(peer(k)), device_id_type=MESH,
        )

    for g in range(GROUP_SPLIT):
        lax.fori_loop(g * step_w, (g + 1) * step_w, whiten, 0)
        for k in range(1, rows):
            share(g, k).start()
    for k in range(1, rows):
        share(GROUP_SPLIT, k).start()

    own = pltpu.make_async_copy(sbuf.at[me], rbuf.at[me], own_sem)
    own.start()

    for t in range(2):
        first = col * half + me * bins + t * part_bins
        freq = first + lax.broadcasted_iota(jnp.int32, (part_bins, LAGS), 0)
        lag = 1 + lax.broadcasted_iota(jnp.int32, (part_bins, LAGS), 1)
        phase = freq * lag
        for p in range(2):
            turn = jnp.bitwise_and(phase + p * (F // 2), 2 * F - 1)
            wave = jnp.cos(turn.astype(jnp.float32) * (math.pi / F)) * (1.0 / math.sqrt(F))
            table[t, p * part_bins:(p + 1) * part_bins, :LAGS] = wave.astype(jnp.bfloat16)
            table[t, p * part_bins:(p + 1) * part_bins, LAGS:] = (wave if p == 0 else -wave).astype(jnp.bfloat16)

    own.wait()

    def widen(source, t):
        def one(w, _):
            both = rbuf[source, t, w].astype(jnp.float32)
            a, b = both[:ch], both[ch:]
            re[source, w] = a
            im[source, w] = b
            su[source, w] = a + b
            di[source, w] = a - b
            return 0

        lax.fori_loop(0, windows, one, 0)

    def arrival(k, source, g):
        if g < GROUP_SPLIT:
            span = pl.ds(g * step_w, step_w)
            target = rbuf.at[source, 0, span]
        else:
            target = rbuf.at[source, 1]
        return pltpu.make_async_remote_copy(
            src_ref=target, dst_ref=target, send_sem=a2a_send.at[g, k], recv_sem=a2a_recv.at[g, k],
            device_id=at_row(peer(k)), device_id_type=MESH,
        )

    def first_half(k, _):
        source = lax.rem(me + rows - k, rows)
        pltpu.make_async_remote_copy(
            src_ref=marks.at[source], dst_ref=marks.at[source], send_sem=mark_send.at[k], recv_sem=mark_recv.at[k],
            device_id=at_row(peer(k)), device_id_type=MESH,
        ).wait_recv()
        for g in range(GROUP_SPLIT):
            arrival(k, source, g).wait_recv()
        widen(source, 0)
        return 0

    def second_half(k, _):
        source = lax.rem(me + rows - k, rows)
        arrival(k, source, GROUP_SPLIT).wait_recv()
        widen(source, 1)
        return 0

    quarter = ch // 2

    def stack(block_i, block_j):
        right = [(re[block_j, w], im[block_j, w], di[block_j, w]) for w in range(windows)]
        real, imag = [], []
        marks_j = marks[block_j]
        for i in range(ch):
            k1 = k2 = k3 = None
            for w in range(windows):
                c, d, e = right[w]
                a = re[block_i, w, i:i + 1, :]
                b = im[block_i, w, i:i + 1, :]
                s = su[block_i, w, i:i + 1, :]
                k1 = a * c if k1 is None else k1 + a * c
                k2 = b * d if k2 is None else k2 + b * d
                k3 = s * e if k3 is None else k3 + s * e
            count = jnp.sum(marks[block_i, i:i + 1, :] * marks_j, axis=1, keepdims=True)
            scale = 1.0 / jnp.maximum(count, 1.0)
            real.append((k1 + k2) * scale)
            imag.append((k3 - k1 + k2) * scale)
        return jnp.concatenate(
            [jnp.concatenate(real, axis=0), jnp.concatenate(imag, axis=0)], axis=1
        ).astype(jnp.bfloat16)

    def pair(block_i, block_j, slot):
        result = jnp.dot(stash[slot], table[0], preferred_element_type=jnp.float32)
        result = result + jnp.dot(stack(block_i, block_j), table[1], preferred_element_type=jnp.float32)
        for i in range(ch):
            tile = result[i * ch:(i + 1) * ch]
            for h in range(2):
                part[h, block_i, i, block_j] = tile[h * quarter:(h + 1) * quarter, :LAGS]
            mirror = tile[:, LAGS:]
            for j in range(ch):
                part[i // quarter, block_j, j, block_i, i % quarter:i % quarter + 1, :] = mirror[j:j + 1, :]

    high, low = lax.div(me, 2), lax.rem(me, 2)

    def owner(n):
        place = lax.rem(high + 1 + lax.div(n, 2), pairs)
        return 2 * place + lax.rem(low + 1 + lax.rem(n, 2), 2)

    def to_mate(n):
        r = owner(n)
        return pltpu.make_async_remote_copy(
            src_ref=part.at[other, r], dst_ref=mate.at[r], send_sem=mate_send.at[n], recv_sem=mate_recv.at[n],
            device_id=at_mate, device_id_type=MESH,
        )

    def fold(n):
        to_mate(n).wait_recv()
        r = owner(n)
        for i in range(ch):
            part[col, r, i] = part[col, r, i] + mate[r, i]

    def to_near(q):
        place = lax.rem(high + 1 + q, pairs)
        return pltpu.make_async_remote_copy(
            src_ref=part.at[col, owner(2 * q)], dst_ref=near.at[place],
            send_sem=near_send.at[q], recv_sem=near_recv.at[q],
            device_id=at_row(2 * high + 1 - low), device_id_type=MESH,
        )

    def to_row(q):
        r = owner(2 * q + 1)
        return pltpu.make_async_remote_copy(
            src_ref=part.at[col, r], dst_ref=got.at[high], send_sem=row_send.at[q], recv_sem=row_recv.at[q],
            device_id=at_row(r), device_id_type=MESH,
        )

    def join(q):
        to_near(q).wait_recv()
        r = owner(2 * q + 1)
        place = lax.rem(high + 1 + q, pairs)
        for i in range(ch):
            part[col, r, i] = part[col, r, i] + near[place, i]

    widen(me, 0)
    lax.fori_loop(1, rows, first_half, 0)

    def early(n, _):
        def inner(m, _):
            stash[n * rows + m] = stack(owner(n), owner(m))
            return 0

        lax.fori_loop(n, rows, inner, 0)
        return 0

    lax.fori_loop(0, rows, early, 0)
    widen(me, 1)
    lax.fori_loop(1, rows, second_half, 0)

    def sweep(n, _):
        def inner(m, _):
            pair(owner(n), owner(m), n * rows + m)
            return 0

        lax.fori_loop(n, rows, inner, 0)
        to_mate(n).start()

        @pl.when(n > 0)
        def _():
            fold(n - 1)

        @pl.when(lax.rem(n, 2) == 1)
        def _():
            to_near(lax.div(n, 2)).start()

        @pl.when(jnp.logical_and(n > 2, lax.rem(n, 2) == 1))
        def _():
            join(lax.div(n, 2) - 1)
            to_row(lax.div(n, 2) - 1).start()

        return 0

    lax.fori_loop(0, rows, sweep, 0)
    fold(rows - 1)
    join(pairs - 1)

    for i in range(ch):
        out_ref[i, 0] = part[col, me, i].reshape(rows * quarter, LAGS)

    def collect(q, _):
        source = lax.rem(high + pairs + pairs - 1 - q, pairs)
        pltpu.make_async_remote_copy(
            src_ref=got.at[source], dst_ref=got.at[source], send_sem=row_send.at[q], recv_sem=row_recv.at[q],
            device_id=at_row(owner(2 * q + 1)), device_id_type=MESH,
        ).wait_recv()
        for i in range(ch):
            out_ref[i, 0] = out_ref[i, 0] + got[source, i].reshape(rows * quarter, LAGS)
        return 0

    lax.fori_loop(0, pairs - 1, collect, 0)
    for k in range(1, rows):
        mark_copy(k).wait_send()
        for g in range(GROUP_SPLIT + 1):
            share(g, k).wait_send()
    for n in range(rows):
        to_mate(n).wait_send()
    for q in range(pairs):
        to_near(q).wait_send()
        if q < pairs - 1:
            to_row(q).wait_send()


def fused(spectra, masks):
    windows, _, ch, half = spectra.shape
    rows = lax.axis_size("row")
    part_bins = half // rows // 2
    pairs = rows // 2
    quarter = ch // 2
    f32, bf16 = jnp.float32, jnp.bfloat16
    dma = pltpu.SemaphoreType.DMA
    return pl.pallas_call(
        functools.partial(kernel, rows),
        out_shape=jax.ShapeDtypeStruct((ch, 1, rows * quarter, LAGS), f32),
        in_specs=[pl.BlockSpec(memory_space=pltpu.VMEM)] * 2,
        out_specs=pl.BlockSpec(memory_space=pltpu.VMEM),
        scratch_shapes=[
            pltpu.VMEM((windows, ch, half + 2 * LANES), f32),
            pltpu.VMEM((windows, ch, LANES), f32),
            pltpu.VMEM((windows, ch, LANES), f32),
            pltpu.VMEM((rows, ch, LANES), f32),
            pltpu.VMEM((windows, ch, LANES), f32),
            pltpu.VMEM((rows, 2, windows, 2 * ch, part_bins), bf16),
            pltpu.VMEM((rows, 2, windows, 2 * ch, part_bins), bf16),
            pltpu.VMEM((rows, windows, ch, part_bins), f32),
            pltpu.VMEM((rows, windows, ch, part_bins), f32),
            pltpu.VMEM((rows, windows, ch, part_bins), f32),
            pltpu.VMEM((rows, windows, ch, part_bins), f32),
            pltpu.VMEM((2, 2 * part_bins, 2 * LAGS), bf16),
            pltpu.VMEM((rows * rows, ch * ch, 2 * part_bins), bf16),
            pltpu.VMEM((2, rows, ch, rows, quarter, LAGS), f32),
            pltpu.VMEM((rows, ch, rows, quarter, LAGS), f32),
            pltpu.VMEM((pairs, ch, rows, quarter, LAGS), f32),
            pltpu.VMEM((pairs, ch, rows, quarter, LAGS), f32),
            dma((2,)),
            dma((rows,)),
            dma((rows,)),
            dma((GROUP_SPLIT + 1, rows)),
            dma((GROUP_SPLIT + 1, rows)),
            dma,
            dma((rows,)),
            dma((rows,)),
            dma((pairs,)),
            dma((pairs,)),
            dma((pairs,)),
            dma((pairs,)),
        ],
        compiler_params=pltpu.CompilerParams(
            collective_id=0, has_side_effects=True, vmem_limit_bytes=48 * 1024 * 1024
        ),
    )(spectra, masks)


def with_halo(cells, width):
    head = cells[..., :width]
    tail = cells[..., cells.shape[-1] - width:]
    return jnp.concatenate(
        [lax.ppermute(tail, "col", [(0, 1)]), cells, lax.ppermute(head, "col", [(1, 0)])], axis=-1
    )


def cosine_table(first, count):
    freqs = first + jnp.arange(count, dtype=jnp.int32)
    shifts = jnp.arange(1, LAGS + 1, dtype=jnp.int32)
    phase = freqs[:, None] * shifts[None, :] % (2 * F)
    angle = jnp.pi * phase.astype(jnp.float32) / F
    factor = 1.0 / math.sqrt(F)
    return jnp.concatenate([jnp.cos(angle) * factor, -jnp.sin(angle) * factor], axis=0).astype(jnp.bfloat16)


def correlate(own, own_live, far, far_live, table):
    a, b = own[:, 0].astype(jnp.float32), own[:, 1].astype(jnp.float32)
    c, d = far[:, 0].astype(jnp.float32), far[:, 1].astype(jnp.float32)
    shape = (own.shape[2], far.shape[2], own.shape[3])
    real = jnp.zeros(shape, jnp.float32)
    imag = jnp.zeros(shape, jnp.float32)
    for w in range(own.shape[0]):
        real = real + (a[w, :, None] * c[w, None] + b[w, :, None] * d[w, None])
        imag = imag + (b[w, :, None] * c[w, None] - a[w, :, None] * d[w, None])
    count = jnp.maximum(jnp.dot(own_live.T, far_live, preferred_element_type=jnp.float32), 1.0)
    stacked = (jnp.stack([real, imag], axis=2) / count[:, :, None, None]).astype(jnp.bfloat16)
    lines = stacked.reshape(shape[0] * shape[1], -1)
    return jnp.dot(lines, table, preferred_element_type=jnp.float32).reshape(shape[0], shape[1], LAGS)


def ring(spectra, masks):
    ch, half = spectra.shape[2], spectra.shape[3]
    rows = lax.axis_size("row")
    me, col = lax.axis_index("row"), lax.axis_index("col")
    quarter = ch // 2
    live = masks.astype(jnp.float32)
    values = spectra.astype(jnp.float32)
    padded = with_halo(jnp.sqrt(values[:, 0] * values[:, 0] + values[:, 1] * values[:, 1]), SMOOTH)
    total = padded
    for by in (1, 2, 4, 8, 16, 32):
        total = total[..., :-by] + total[..., by:]
    total = total[..., :half] + padded[..., 2 * SMOOTH:]
    amplitude = total / (2 * SMOOTH + 1) + EPSILON
    whitened = (values / amplitude[:, None] * live[:, None, :, None]).astype(jnp.bfloat16)
    table = cosine_table(col * half, half)
    onward = [(r, (r + 1) % rows) for r in range(rows)]

    def step(n, carry):
        result, far, marks = carry
        block = correlate(whitened, live, far, marks.astype(jnp.float32), table)
        block = block.reshape(ch, 2, quarter, LAGS)
        source = lax.rem(me + rows - n, rows)
        result = lax.dynamic_update_slice(result, block, (0, 0, source * quarter, 0))
        return result, lax.ppermute(far, "row", onward), lax.ppermute(marks, "row", onward)

    empty = jnp.zeros((ch, 2, rows * quarter, LAGS), jnp.float32)
    result, _, _ = lax.fori_loop(0, rows, step, (empty, whitened, live.astype(jnp.bfloat16)))
    mine = lax.dynamic_slice_in_dim(result, col, 1, 1)
    other = lax.dynamic_slice_in_dim(result, 1 - col, 1, 1)
    return mine + lax.ppermute(other, "col", [(0, 1), (1, 0)])


def per_device(spectra, masks):
    windows, _, ch, half = spectra.shape
    rows = lax.axis_size("row")
    bins = half // rows
    fits = rows in (2, 4, 6, 8) and ch == 8 and bins % (2 * LANES) == 0 and windows % GROUP_SPLIT == 0 and windows <= LANES
    return fused(spectra, masks) if fits else ring(spectra, masks)


def solution(mesh):
    return jax.shard_map(
        per_device,
        mesh=mesh,
        in_specs=(P("hours", None, "row", "col"), P("hours", "row")),
        out_specs=P(("hours", "row"), "col", None, None),
        check_vma=False,
    )
```

```python
import functools
import math

import jax
import jax.numpy as jnp
from jax import lax
from jax.experimental import pallas as pl
from jax.experimental.pallas import tpu as pltpu
from jax.sharding import PartitionSpec as P

F = 4096
SMOOTH = 32
LAGS = 128
EPSILON = 1e-05
LANES = 128
GROUP_SPLIT = 6
MESH = pl.DeviceIdType.MESH


def shifted(cells, by):
    return pltpu.roll(cells, (-by) % cells.shape[1], 1)


def kernel(
    rows, x_ref, m_ref, out_ref,
    mag, halo_out, halo_in, marks, live, sbuf, rbuf, re, im, su, di, table, stash, part, mate, near, got,
    halo_sem, mark_send, mark_recv, a2a_send, a2a_recv, own_sem, mate_send, mate_recv, near_send, near_recv, row_send, row_recv,
):
    windows, _, ch, half = x_ref.shape
    bins = half // rows
    part_bins = bins // 2
    pairs = rows // 2
    hours, me, col = lax.axis_index("hours"), lax.axis_index("row"), lax.axis_index("col")
    other = 1 - col
    step_w = windows // GROUP_SPLIT

    def peer(k):
        return lax.rem(me + k, rows)

    def at_row(r):
        return (hours, r, col)

    at_mate = (hours, me, other)

    barrier = pltpu.get_barrier_semaphore()
    for k in range(1, rows):
        pl.semaphore_signal(barrier, inc=1, device_id=at_row(peer(k)), device_id_type=MESH)
    pl.semaphore_signal(barrier, inc=1, device_id=at_mate, device_id_type=MESH)

    def magnitude(a, b):
        return jnp.sqrt(a * a + b * b)

    def edges(w, _):
        a = x_ref[w, 0, :, half - LANES:].astype(jnp.float32)
        b = x_ref[w, 1, :, half - LANES:].astype(jnp.float32)
        c = x_ref[w, 0, :, :LANES].astype(jnp.float32)
        d = x_ref[w, 1, :, :LANES].astype(jnp.float32)
        first = col == 0
        halo_out[w] = magnitude(jnp.where(first, a, c), jnp.where(first, b, d))
        return 0

    lax.fori_loop(0, windows, edges, 0)

    lane = lax.broadcasted_iota(jnp.int32, (ch, LANES), 1)
    diag = lax.broadcasted_iota(jnp.int32, (ch, ch), 0) == lax.broadcasted_iota(jnp.int32, (ch, ch), 1)
    packed = jnp.zeros((ch, LANES), jnp.float32)
    for w in range(windows):
        row = m_ref[w:w + 1, :].astype(jnp.float32)
        column = jnp.sum(jnp.where(diag, row, 0.0), axis=1, keepdims=True)
        wide = jnp.broadcast_to(column, (ch, LANES))
        live[w] = wide
        packed = jnp.where(lane == w, wide, packed)
    marks[me] = packed

    def fill(w, _):
        a = x_ref[w, 0].astype(jnp.float32)
        b = x_ref[w, 1].astype(jnp.float32)
        mag[w, :, LANES:LANES + half] = magnitude(a, b)
        return 0

    lax.fori_loop(0, windows, fill, 0)
    pl.semaphore_wait(barrier, rows)

    halo = pltpu.make_async_remote_copy(
        src_ref=halo_out, dst_ref=halo_in, send_sem=halo_sem.at[0], recv_sem=halo_sem.at[1],
        device_id=at_mate, device_id_type=MESH,
    )
    halo.start()

    def mark_copy(k):
        return pltpu.make_async_remote_copy(
            src_ref=marks.at[me], dst_ref=marks.at[me], send_sem=mark_send.at[k], recv_sem=mark_recv.at[k],
            device_id=at_row(peer(k)), device_id_type=MESH,
        )

    for k in range(1, rows):
        mark_copy(k).start()

    halo.wait()

    def whiten(w, _):
        edge = halo_in[w]
        zero = jnp.zeros_like(edge)
        cells = jnp.concatenate(
            [jnp.where(col == 0, zero, edge), mag[w, :, LANES:LANES + half], jnp.where(col == 0, edge, zero)], axis=1
        )
        total = cells
        for by in (1, 2, 4, 8, 16):
            total = total + shifted(total, by)
        total = total + shifted(total, -SMOOTH) + shifted(cells, SMOOTH)
        total = total[:, LANES:LANES + half]
        amplitude = total / (2 * SMOOTH + 1) + EPSILON
        scale = live[w][:, :1] / amplitude
        both = jnp.concatenate(
            [x_ref[w, 0].astype(jnp.float32) * scale, x_ref[w, 1].astype(jnp.float32) * scale], axis=0
        ).astype(jnp.bfloat16)
        for r in range(rows):
            for t in range(2):
                start = r * bins + t * part_bins
                sbuf[r, t, w] = both[:, start:start + part_bins]
        return 0

    def share(g, k):
        if g < GROUP_SPLIT:
            span = pl.ds(g * step_w, step_w)
            source, target = sbuf.at[peer(k), 0, span], rbuf.at[me, 0, span]
        else:
            source, target = sbuf.at[peer(k), 1], rbuf.at[me, 1]
        return pltpu.make_async_remote_copy(
            src_ref=source, dst_ref=target, send_sem=a2a_send.at[g, k], recv_sem=a2a_recv.at[g, k],
            device_id=at_row(peer(k)), device_id_type=MESH,
        )

    order = sorted(range(1, rows), key=lambda k: abs(2 * k - rows))
    for g in range(GROUP_SPLIT):
        lax.fori_loop(g * step_w, (g + 1) * step_w, whiten, 0)
        for k in order:
            share(g, k).start()
    for k in order:
        share(GROUP_SPLIT, k).start()

    own = pltpu.make_async_copy(sbuf.at[me], rbuf.at[me], own_sem)
    own.start()

    for t in range(2):
        first = col * half + me * bins + t * part_bins
        freq = first + lax.broadcasted_iota(jnp.int32, (part_bins, LAGS), 0)
        lag = 1 + lax.broadcasted_iota(jnp.int32, (part_bins, LAGS), 1)
        phase = freq * lag
        for p in range(2):
            turn = jnp.bitwise_and(phase + p * (F // 2), 2 * F - 1)
            wave = jnp.cos(turn.astype(jnp.float32) * (math.pi / F)) * (1.0 / math.sqrt(F))
            table[t, p * part_bins:(p + 1) * part_bins, :LAGS] = wave.astype(jnp.bfloat16)
            table[t, p * part_bins:(p + 1) * part_bins, LAGS:] = (wave if p == 0 else -wave).astype(jnp.bfloat16)

    own.wait()

    def widen(source, t):
        def one(w, _):
            both = rbuf[source, t, w].astype(jnp.float32)
            a, b = both[:ch], both[ch:]
            re[source, w] = a
            im[source, w] = b
            su[source, w] = a + b
            di[source, w] = a - b
            return 0

        lax.fori_loop(0, windows, one, 0)

    def arrival(k, source, g):
        if g < GROUP_SPLIT:
            span = pl.ds(g * step_w, step_w)
            target = rbuf.at[source, 0, span]
        else:
            target = rbuf.at[source, 1]
        return pltpu.make_async_remote_copy(
            src_ref=target, dst_ref=target, send_sem=a2a_send.at[g, k], recv_sem=a2a_recv.at[g, k],
            device_id=at_row(peer(k)), device_id_type=MESH,
        )

    def first_half(k, _):
        source = lax.rem(me + rows - k, rows)
        pltpu.make_async_remote_copy(
            src_ref=marks.at[source], dst_ref=marks.at[source], send_sem=mark_send.at[k], recv_sem=mark_recv.at[k],
            device_id=at_row(peer(k)), device_id_type=MESH,
        ).wait_recv()
        for g in range(GROUP_SPLIT):
            arrival(k, source, g).wait_recv()
        widen(source, 0)
        return 0

    def second_half(k, _):
        source = lax.rem(me + rows - k, rows)
        arrival(k, source, GROUP_SPLIT).wait_recv()
        widen(source, 1)
        return 0

    quarter = ch // 2

    def stack(block_i, block_j):
        right = [(re[block_j, w], im[block_j, w], di[block_j, w]) for w in range(windows)]
        real, imag = [], []
        marks_j = marks[block_j]
        for i in range(ch):
            k1 = k2 = k3 = None
            for w in range(windows):
                c, d, e = right[w]
                a = re[block_i, w, i:i + 1, :]
                b = im[block_i, w, i:i + 1, :]
                s = su[block_i, w, i:i + 1, :]
                k1 = a * c if k1 is None else k1 + a * c
                k2 = b * d if k2 is None else k2 + b * d
                k3 = s * e if k3 is None else k3 + s * e
            count = jnp.sum(marks[block_i, i:i + 1, :] * marks_j, axis=1, keepdims=True)
            scale = 1.0 / jnp.maximum(count, 1.0)
            real.append((k1 + k2) * scale)
            imag.append((k3 - k1 + k2) * scale)
        return jnp.concatenate(
            [jnp.concatenate(real, axis=0), jnp.concatenate(imag, axis=0)], axis=1
        ).astype(jnp.bfloat16)

    def pair(block_i, block_j, slot):
        result = jnp.dot(stash[slot], table[0], preferred_element_type=jnp.float32)
        result = result + jnp.dot(stack(block_i, block_j), table[1], preferred_element_type=jnp.float32)
        for i in range(ch):
            tile = result[i * ch:(i + 1) * ch]
            for h in range(2):
                part[h, block_i, i, block_j] = tile[h * quarter:(h + 1) * quarter, :LAGS]
            mirror = tile[:, LAGS:]
            for j in range(ch):
                part[i // quarter, block_j, j, block_i, i % quarter:i % quarter + 1, :] = mirror[j:j + 1, :]

    high, low = lax.div(me, 2), lax.rem(me, 2)

    def owner(n):
        place = lax.rem(high + 1 + lax.div(n, 2), pairs)
        return 2 * place + lax.rem(low + 1 + lax.rem(n, 2), 2)

    def to_mate(n):
        r = owner(n)
        return pltpu.make_async_remote_copy(
            src_ref=part.at[other, r], dst_ref=mate.at[r], send_sem=mate_send.at[n], recv_sem=mate_recv.at[n],
            device_id=at_mate, device_id_type=MESH,
        )

    def fold(n):
        to_mate(n).wait_recv()
        r = owner(n)
        for i in range(ch):
            part[col, r, i] = part[col, r, i] + mate[r, i]

    def to_near(q):
        place = lax.rem(high + 1 + q, pairs)
        return pltpu.make_async_remote_copy(
            src_ref=part.at[col, owner(2 * q)], dst_ref=near.at[place],
            send_sem=near_send.at[q], recv_sem=near_recv.at[q],
            device_id=at_row(2 * high + 1 - low), device_id_type=MESH,
        )

    def to_row(q):
        r = owner(2 * q + 1)
        return pltpu.make_async_remote_copy(
            src_ref=part.at[col, r], dst_ref=got.at[high], send_sem=row_send.at[q], recv_sem=row_recv.at[q],
            device_id=at_row(r), device_id_type=MESH,
        )

    def join(q):
        to_near(q).wait_recv()
        r = owner(2 * q + 1)
        place = lax.rem(high + 1 + q, pairs)
        for i in range(ch):
            part[col, r, i] = part[col, r, i] + near[place, i]

    widen(me, 0)
    lax.fori_loop(1, rows, first_half, 0)

    def early(n, _):
        def inner(m, _):
            stash[n * rows + m] = stack(owner(n), owner(m))
            return 0

        lax.fori_loop(n, rows, inner, 0)
        return 0

    lax.fori_loop(0, rows, early, 0)
    widen(me, 1)
    lax.fori_loop(1, rows, second_half, 0)

    def sweep(n, _):
        def inner(m, _):
            pair(owner(n), owner(m), n * rows + m)
            return 0

        lax.fori_loop(n, rows, inner, 0)
        to_mate(n).start()

        @pl.when(n > 0)
        def _():
            fold(n - 1)

        @pl.when(lax.rem(n, 2) == 1)
        def _():
            to_near(lax.div(n, 2)).start()

        @pl.when(jnp.logical_and(n > 2, lax.rem(n, 2) == 1))
        def _():
            join(lax.div(n, 2) - 1)
            to_row(lax.div(n, 2) - 1).start()

        return 0

    lax.fori_loop(0, rows, sweep, 0)
    fold(rows - 1)
    join(pairs - 1)

    for i in range(ch):
        out_ref[i, 0] = part[col, me, i].reshape(rows * quarter, LAGS)

    def collect(q, _):
        source = lax.rem(high + pairs + pairs - 1 - q, pairs)
        pltpu.make_async_remote_copy(
            src_ref=got.at[source], dst_ref=got.at[source], send_sem=row_send.at[q], recv_sem=row_recv.at[q],
            device_id=at_row(owner(2 * q + 1)), device_id_type=MESH,
        ).wait_recv()
        for i in range(ch):
            out_ref[i, 0] = out_ref[i, 0] + got[source, i].reshape(rows * quarter, LAGS)
        return 0

    lax.fori_loop(0, pairs - 1, collect, 0)
    for k in range(1, rows):
        mark_copy(k).wait_send()
        for g in range(GROUP_SPLIT + 1):
            share(g, k).wait_send()
    for n in range(rows):
        to_mate(n).wait_send()
    for q in range(pairs):
        to_near(q).wait_send()
        if q < pairs - 1:
            to_row(q).wait_send()


def fused(spectra, masks):
    windows, _, ch, half = spectra.shape
    rows = lax.axis_size("row")
    part_bins = half // rows // 2
    pairs = rows // 2
    quarter = ch // 2
    f32, bf16 = jnp.float32, jnp.bfloat16
    dma = pltpu.SemaphoreType.DMA
    return pl.pallas_call(
        functools.partial(kernel, rows),
        out_shape=jax.ShapeDtypeStruct((ch, 1, rows * quarter, LAGS), f32),
        in_specs=[pl.BlockSpec(memory_space=pltpu.VMEM)] * 2,
        out_specs=pl.BlockSpec(memory_space=pltpu.VMEM),
        scratch_shapes=[
            pltpu.VMEM((windows, ch, half + 2 * LANES), f32),
            pltpu.VMEM((windows, ch, LANES), f32),
            pltpu.VMEM((windows, ch, LANES), f32),
            pltpu.VMEM((rows, ch, LANES), f32),
            pltpu.VMEM((windows, ch, LANES), f32),
            pltpu.VMEM((rows, 2, windows, 2 * ch, part_bins), bf16),
            pltpu.VMEM((rows, 2, windows, 2 * ch, part_bins), bf16),
            pltpu.VMEM((rows, windows, ch, part_bins), f32),
            pltpu.VMEM((rows, windows, ch, part_bins), f32),
            pltpu.VMEM((rows, windows, ch, part_bins), f32),
            pltpu.VMEM((rows, windows, ch, part_bins), f32),
            pltpu.VMEM((2, 2 * part_bins, 2 * LAGS), bf16),
            pltpu.VMEM((rows * rows, ch * ch, 2 * part_bins), bf16),
            pltpu.VMEM((2, rows, ch, rows, quarter, LAGS), f32),
            pltpu.VMEM((rows, ch, rows, quarter, LAGS), f32),
            pltpu.VMEM((pairs, ch, rows, quarter, LAGS), f32),
            pltpu.VMEM((pairs, ch, rows, quarter, LAGS), f32),
            dma((2,)),
            dma((rows,)),
            dma((rows,)),
            dma((GROUP_SPLIT + 1, rows)),
            dma((GROUP_SPLIT + 1, rows)),
            dma,
            dma((rows,)),
            dma((rows,)),
            dma((pairs,)),
            dma((pairs,)),
            dma((pairs,)),
            dma((pairs,)),
        ],
        compiler_params=pltpu.CompilerParams(
            collective_id=0, has_side_effects=True, vmem_limit_bytes=48 * 1024 * 1024
        ),
    )(spectra, masks)


def with_halo(cells, width):
    head = cells[..., :width]
    tail = cells[..., cells.shape[-1] - width:]
    return jnp.concatenate(
        [lax.ppermute(tail, "col", [(0, 1)]), cells, lax.ppermute(head, "col", [(1, 0)])], axis=-1
    )


def cosine_table(first, count):
    freqs = first + jnp.arange(count, dtype=jnp.int32)
    shifts = jnp.arange(1, LAGS + 1, dtype=jnp.int32)
    phase = freqs[:, None] * shifts[None, :] % (2 * F)
    angle = jnp.pi * phase.astype(jnp.float32) / F
    factor = 1.0 / math.sqrt(F)
    return jnp.concatenate([jnp.cos(angle) * factor, -jnp.sin(angle) * factor], axis=0).astype(jnp.bfloat16)


def correlate(own, own_live, far, far_live, table):
    a, b = own[:, 0].astype(jnp.float32), own[:, 1].astype(jnp.float32)
    c, d = far[:, 0].astype(jnp.float32), far[:, 1].astype(jnp.float32)
    shape = (own.shape[2], far.shape[2], own.shape[3])
    real = jnp.zeros(shape, jnp.float32)
    imag = jnp.zeros(shape, jnp.float32)
    for w in range(own.shape[0]):
        real = real + (a[w, :, None] * c[w, None] + b[w, :, None] * d[w, None])
        imag = imag + (b[w, :, None] * c[w, None] - a[w, :, None] * d[w, None])
    count = jnp.maximum(jnp.dot(own_live.T, far_live, preferred_element_type=jnp.float32), 1.0)
    stacked = (jnp.stack([real, imag], axis=2) / count[:, :, None, None]).astype(jnp.bfloat16)
    lines = stacked.reshape(shape[0] * shape[1], -1)
    return jnp.dot(lines, table, preferred_element_type=jnp.float32).reshape(shape[0], shape[1], LAGS)


def ring(spectra, masks):
    ch, half = spectra.shape[2], spectra.shape[3]
    rows = lax.axis_size("row")
    me, col = lax.axis_index("row"), lax.axis_index("col")
    quarter = ch // 2
    live = masks.astype(jnp.float32)
    values = spectra.astype(jnp.float32)
    padded = with_halo(jnp.sqrt(values[:, 0] * values[:, 0] + values[:, 1] * values[:, 1]), SMOOTH)
    total = padded
    for by in (1, 2, 4, 8, 16, 32):
        total = total[..., :-by] + total[..., by:]
    total = total[..., :half] + padded[..., 2 * SMOOTH:]
    amplitude = total / (2 * SMOOTH + 1) + EPSILON
    whitened = (values / amplitude[:, None] * live[:, None, :, None]).astype(jnp.bfloat16)
    table = cosine_table(col * half, half)
    onward = [(r, (r + 1) % rows) for r in range(rows)]

    def step(n, carry):
        result, far, marks = carry
        block = correlate(whitened, live, far, marks.astype(jnp.float32), table)
        block = block.reshape(ch, 2, quarter, LAGS)
        source = lax.rem(me + rows - n, rows)
        result = lax.dynamic_update_slice(result, block, (0, 0, source * quarter, 0))
        return result, lax.ppermute(far, "row", onward), lax.ppermute(marks, "row", onward)

    empty = jnp.zeros((ch, 2, rows * quarter, LAGS), jnp.float32)
    result, _, _ = lax.fori_loop(0, rows, step, (empty, whitened, live.astype(jnp.bfloat16)))
    mine = lax.dynamic_slice_in_dim(result, col, 1, 1)
    other = lax.dynamic_slice_in_dim(result, 1 - col, 1, 1)
    return mine + lax.ppermute(other, "col", [(0, 1), (1, 0)])


def per_device(spectra, masks):
    windows, _, ch, half = spectra.shape
    rows = lax.axis_size("row")
    bins = half // rows
    fits = rows in (2, 4, 6, 8) and ch == 8 and bins % (2 * LANES) == 0 and windows % GROUP_SPLIT == 0 and windows <= LANES
    return fused(spectra, masks) if fits else ring(spectra, masks)


def solution(mesh):
    return jax.shard_map(
        per_device,
        mesh=mesh,
        in_specs=(P("hours", None, "row", "col"), P("hours", "row")),
        out_specs=P(("hours", "row"), "col", None, None),
        check_vma=False,
    )
```

```python
import functools
import math

import jax
import jax.numpy as jnp
from jax import lax
from jax.experimental import pallas as pl
from jax.experimental.pallas import tpu as pltpu
from jax.sharding import PartitionSpec as P

F = 4096
SMOOTH = 32
LAGS = 128
EPSILON = 1e-05
LANES = 128
GROUP_SPLIT = 6
MESH = pl.DeviceIdType.MESH


def shifted(cells, by):
    return pltpu.roll(cells, (-by) % cells.shape[1], 1)


def kernel(
    rows, x_ref, m_ref, out_ref,
    mag, halo_out, halo_in, marks, live, sbuf, rbuf, re, im, su, di, table, stash, part, mate, near, got,
    halo_sem, mark_send, mark_recv, a2a_send, a2a_recv, own_sem, mate_send, mate_recv, near_send, near_recv, row_send, row_recv,
):
    windows, _, ch, half = x_ref.shape
    bins = half // rows
    part_bins = bins // 2
    pairs = rows // 2
    hours, me, col = lax.axis_index("hours"), lax.axis_index("row"), lax.axis_index("col")
    other = 1 - col
    step_w = windows // GROUP_SPLIT

    def peer(k):
        return lax.rem(me + k, rows)

    def at_row(r):
        return (hours, r, col)

    at_mate = (hours, me, other)

    barrier = pltpu.get_barrier_semaphore()
    for k in range(1, rows):
        pl.semaphore_signal(barrier, inc=1, device_id=at_row(peer(k)), device_id_type=MESH)
    pl.semaphore_signal(barrier, inc=1, device_id=at_mate, device_id_type=MESH)

    def magnitude(a, b):
        return jnp.sqrt(a * a + b * b)

    def edges(w, _):
        a = x_ref[w, 0, :, half - LANES:].astype(jnp.float32)
        b = x_ref[w, 1, :, half - LANES:].astype(jnp.float32)
        c = x_ref[w, 0, :, :LANES].astype(jnp.float32)
        d = x_ref[w, 1, :, :LANES].astype(jnp.float32)
        first = col == 0
        halo_out[w] = magnitude(jnp.where(first, a, c), jnp.where(first, b, d))
        return 0

    lax.fori_loop(0, windows, edges, 0, unroll=4)

    lane = lax.broadcasted_iota(jnp.int32, (ch, LANES), 1)
    diag = lax.broadcasted_iota(jnp.int32, (ch, ch), 0) == lax.broadcasted_iota(jnp.int32, (ch, ch), 1)
    packed = jnp.zeros((ch, LANES), jnp.float32)
    for w in range(windows):
        row = m_ref[w:w + 1, :].astype(jnp.float32)
        column = jnp.sum(jnp.where(diag, row, 0.0), axis=1, keepdims=True)
        wide = jnp.broadcast_to(column, (ch, LANES))
        live[w] = wide
        packed = jnp.where(lane == w, wide, packed)
    marks[me] = packed

    def fill(w, _):
        a = x_ref[w, 0].astype(jnp.float32)
        b = x_ref[w, 1].astype(jnp.float32)
        mag[w, :, LANES:LANES + half] = magnitude(a, b)
        return 0

    lax.fori_loop(0, windows, fill, 0, unroll=2)
    pl.semaphore_wait(barrier, rows)

    halo = pltpu.make_async_remote_copy(
        src_ref=halo_out, dst_ref=halo_in, send_sem=halo_sem.at[0], recv_sem=halo_sem.at[1],
        device_id=at_mate, device_id_type=MESH,
    )
    halo.start()

    def mark_copy(k):
        return pltpu.make_async_remote_copy(
            src_ref=marks.at[me], dst_ref=marks.at[me], send_sem=mark_send.at[k], recv_sem=mark_recv.at[k],
            device_id=at_row(peer(k)), device_id_type=MESH,
        )

    for k in range(1, rows):
        mark_copy(k).start()

    halo.wait()

    def whiten(w, _):
        edge = halo_in[w]
        zero = jnp.zeros_like(edge)
        cells = jnp.concatenate(
            [jnp.where(col == 0, zero, edge), mag[w, :, LANES:LANES + half], jnp.where(col == 0, edge, zero)], axis=1
        )
        total = cells
        for by in (1, 2, 4, 8, 16):
            total = total + shifted(total, by)
        total = total + shifted(total, -SMOOTH) + shifted(cells, SMOOTH)
        total = total[:, LANES:LANES + half]
        amplitude = total / (2 * SMOOTH + 1) + EPSILON
        scale = live[w][:, :1] / amplitude
        both = jnp.concatenate(
            [x_ref[w, 0].astype(jnp.float32) * scale, x_ref[w, 1].astype(jnp.float32) * scale], axis=0
        ).astype(jnp.bfloat16)
        for r in range(rows):
            for t in range(2):
                start = r * bins + t * part_bins
                sbuf[r, t, w] = both[:, start:start + part_bins]
        return 0

    def share(g, k):
        if g < GROUP_SPLIT:
            span = pl.ds(g * step_w, step_w)
            source, target = sbuf.at[peer(k), 0, span], rbuf.at[me, 0, span]
        else:
            source, target = sbuf.at[peer(k), 1], rbuf.at[me, 1]
        return pltpu.make_async_remote_copy(
            src_ref=source, dst_ref=target, send_sem=a2a_send.at[g, k], recv_sem=a2a_recv.at[g, k],
            device_id=at_row(peer(k)), device_id_type=MESH,
        )

    order = sorted(range(1, rows), key=lambda k: abs(2 * k - rows))
    for g in range(GROUP_SPLIT):
        lax.fori_loop(g * step_w, (g + 1) * step_w, whiten, 0, unroll=True)
        for k in order:
            share(g, k).start()
    for k in order:
        share(GROUP_SPLIT, k).start()

    own = pltpu.make_async_copy(sbuf.at[me], rbuf.at[me], own_sem)
    own.start()

    for t in range(2):
        first = col * half + me * bins + t * part_bins
        freq = first + lax.broadcasted_iota(jnp.int32, (part_bins, LAGS), 0)
        lag = 1 + lax.broadcasted_iota(jnp.int32, (part_bins, LAGS), 1)
        phase = freq * lag
        for p in range(2):
            turn = jnp.bitwise_and(phase + p * (F // 2), 2 * F - 1)
            wave = jnp.cos(turn.astype(jnp.float32) * (math.pi / F)) * (1.0 / math.sqrt(F))
            table[t, p * part_bins:(p + 1) * part_bins, :LAGS] = wave.astype(jnp.bfloat16)
            table[t, p * part_bins:(p + 1) * part_bins, LAGS:] = (wave if p == 0 else -wave).astype(jnp.bfloat16)

    own.wait()

    def widen(source, t):
        def one(w, _):
            both = rbuf[source, t, w].astype(jnp.float32)
            a, b = both[:ch], both[ch:]
            re[source, w] = a
            im[source, w] = b
            su[source, w] = a + b
            di[source, w] = a - b
            return 0

        lax.fori_loop(0, windows, one, 0, unroll=True)

    def arrival(k, source, g):
        if g < GROUP_SPLIT:
            span = pl.ds(g * step_w, step_w)
            target = rbuf.at[source, 0, span]
        else:
            target = rbuf.at[source, 1]
        return pltpu.make_async_remote_copy(
            src_ref=target, dst_ref=target, send_sem=a2a_send.at[g, k], recv_sem=a2a_recv.at[g, k],
            device_id=at_row(peer(k)), device_id_type=MESH,
        )

    def first_half(k, _):
        source = lax.rem(me + rows - k, rows)
        pltpu.make_async_remote_copy(
            src_ref=marks.at[source], dst_ref=marks.at[source], send_sem=mark_send.at[k], recv_sem=mark_recv.at[k],
            device_id=at_row(peer(k)), device_id_type=MESH,
        ).wait_recv()
        for g in range(GROUP_SPLIT):
            arrival(k, source, g).wait_recv()
        widen(source, 0)
        return 0

    def second_half(k, _):
        source = lax.rem(me + rows - k, rows)
        arrival(k, source, GROUP_SPLIT).wait_recv()
        widen(source, 1)
        return 0

    quarter = ch // 2

    def stack(block_i, block_j):
        right = [(re[block_j, w], im[block_j, w], di[block_j, w]) for w in range(windows)]
        real, imag = [], []
        marks_j = marks[block_j]
        for i in range(ch):
            k1 = k2 = k3 = None
            for w in range(windows):
                c, d, e = right[w]
                a = re[block_i, w, i:i + 1, :]
                b = im[block_i, w, i:i + 1, :]
                s = su[block_i, w, i:i + 1, :]
                k1 = a * c if k1 is None else k1 + a * c
                k2 = b * d if k2 is None else k2 + b * d
                k3 = s * e if k3 is None else k3 + s * e
            count = jnp.sum(marks[block_i, i:i + 1, :] * marks_j, axis=1, keepdims=True)
            scale = 1.0 / jnp.maximum(count, 1.0)
            real.append((k1 + k2) * scale)
            imag.append((k3 - k1 + k2) * scale)
        return jnp.concatenate(
            [jnp.concatenate(real, axis=0), jnp.concatenate(imag, axis=0)], axis=1
        ).astype(jnp.bfloat16)

    def pair(block_i, block_j, slot):
        result = jnp.dot(stash[slot], table[0], preferred_element_type=jnp.float32)
        result = result + jnp.dot(stack(block_i, block_j), table[1], preferred_element_type=jnp.float32)
        for i in range(ch):
            tile = result[i * ch:(i + 1) * ch]
            for h in range(2):
                part[h, block_i, i, block_j] = tile[h * quarter:(h + 1) * quarter, :LAGS]
            mirror = tile[:, LAGS:]
            for j in range(ch):
                part[i // quarter, block_j, j, block_i, i % quarter:i % quarter + 1, :] = mirror[j:j + 1, :]

    high, low = lax.div(me, 2), lax.rem(me, 2)

    def owner(n):
        place = lax.rem(high + 1 + lax.div(n, 2), pairs)
        return 2 * place + lax.rem(low + 1 + lax.rem(n, 2), 2)

    def to_mate(n):
        r = owner(n)
        return pltpu.make_async_remote_copy(
            src_ref=part.at[other, r], dst_ref=mate.at[r], send_sem=mate_send.at[n], recv_sem=mate_recv.at[n],
            device_id=at_mate, device_id_type=MESH,
        )

    def fold(n):
        to_mate(n).wait_recv()
        r = owner(n)
        for i in range(ch):
            part[col, r, i] = part[col, r, i] + mate[r, i]

    def to_near(q):
        place = lax.rem(high + 1 + q, pairs)
        return pltpu.make_async_remote_copy(
            src_ref=part.at[col, owner(2 * q)], dst_ref=near.at[place],
            send_sem=near_send.at[q], recv_sem=near_recv.at[q],
            device_id=at_row(2 * high + 1 - low), device_id_type=MESH,
        )

    def to_row(q):
        r = owner(2 * q + 1)
        return pltpu.make_async_remote_copy(
            src_ref=part.at[col, r], dst_ref=got.at[high], send_sem=row_send.at[q], recv_sem=row_recv.at[q],
            device_id=at_row(r), device_id_type=MESH,
        )

    def join(q):
        to_near(q).wait_recv()
        r = owner(2 * q + 1)
        place = lax.rem(high + 1 + q, pairs)
        for i in range(ch):
            part[col, r, i] = part[col, r, i] + near[place, i]

    widen(me, 0)
    lax.fori_loop(1, rows, first_half, 0)

    def early(n, _):
        def inner(m, _):
            stash[n * rows + m] = stack(owner(n), owner(m))
            return 0

        lax.fori_loop(n, rows, inner, 0)
        return 0

    lax.fori_loop(0, rows, early, 0)
    widen(me, 1)
    lax.fori_loop(1, rows, second_half, 0)

    def sweep(n, _):
        def inner(m, _):
            pair(owner(n), owner(m), n * rows + m)
            return 0

        lax.fori_loop(n, rows, inner, 0)
        to_mate(n).start()

        @pl.when(n > 0)
        def _():
            fold(n - 1)

        @pl.when(lax.rem(n, 2) == 1)
        def _():
            to_near(lax.div(n, 2)).start()

        @pl.when(jnp.logical_and(n > 2, lax.rem(n, 2) == 1))
        def _():
            join(lax.div(n, 2) - 1)
            to_row(lax.div(n, 2) - 1).start()

        return 0

    lax.fori_loop(0, rows, sweep, 0)
    fold(rows - 1)
    join(pairs - 1)

    for i in range(ch):
        out_ref[i, 0] = part[col, me, i].reshape(rows * quarter, LAGS)

    def collect(q, _):
        source = lax.rem(high + pairs + pairs - 1 - q, pairs)
        pltpu.make_async_remote_copy(
            src_ref=got.at[source], dst_ref=got.at[source], send_sem=row_send.at[q], recv_sem=row_recv.at[q],
            device_id=at_row(owner(2 * q + 1)), device_id_type=MESH,
        ).wait_recv()
        for i in range(ch):
            out_ref[i, 0] = out_ref[i, 0] + got[source, i].reshape(rows * quarter, LAGS)
        return 0

    lax.fori_loop(0, pairs - 1, collect, 0)
    for k in range(1, rows):
        mark_copy(k).wait_send()
        for g in range(GROUP_SPLIT + 1):
            share(g, k).wait_send()
    for n in range(rows):
        to_mate(n).wait_send()
    for q in range(pairs):
        to_near(q).wait_send()
        if q < pairs - 1:
            to_row(q).wait_send()


def fused(spectra, masks):
    windows, _, ch, half = spectra.shape
    rows = lax.axis_size("row")
    part_bins = half // rows // 2
    pairs = rows // 2
    quarter = ch // 2
    f32, bf16 = jnp.float32, jnp.bfloat16
    dma = pltpu.SemaphoreType.DMA
    return pl.pallas_call(
        functools.partial(kernel, rows),
        out_shape=jax.ShapeDtypeStruct((ch, 1, rows * quarter, LAGS), f32),
        in_specs=[pl.BlockSpec(memory_space=pltpu.VMEM)] * 2,
        out_specs=pl.BlockSpec(memory_space=pltpu.VMEM),
        scratch_shapes=[
            pltpu.VMEM((windows, ch, half + 2 * LANES), f32),
            pltpu.VMEM((windows, ch, LANES), f32),
            pltpu.VMEM((windows, ch, LANES), f32),
            pltpu.VMEM((rows, ch, LANES), f32),
            pltpu.VMEM((windows, ch, LANES), f32),
            pltpu.VMEM((rows, 2, windows, 2 * ch, part_bins), bf16),
            pltpu.VMEM((rows, 2, windows, 2 * ch, part_bins), bf16),
            pltpu.VMEM((rows, windows, ch, part_bins), f32),
            pltpu.VMEM((rows, windows, ch, part_bins), f32),
            pltpu.VMEM((rows, windows, ch, part_bins), f32),
            pltpu.VMEM((rows, windows, ch, part_bins), f32),
            pltpu.VMEM((2, 2 * part_bins, 2 * LAGS), bf16),
            pltpu.VMEM((rows * rows, ch * ch, 2 * part_bins), bf16),
            pltpu.VMEM((2, rows, ch, rows, quarter, LAGS), f32),
            pltpu.VMEM((rows, ch, rows, quarter, LAGS), f32),
            pltpu.VMEM((pairs, ch, rows, quarter, LAGS), f32),
            pltpu.VMEM((pairs, ch, rows, quarter, LAGS), f32),
            dma((2,)),
            dma((rows,)),
            dma((rows,)),
            dma((GROUP_SPLIT + 1, rows)),
            dma((GROUP_SPLIT + 1, rows)),
            dma,
            dma((rows,)),
            dma((rows,)),
            dma((pairs,)),
            dma((pairs,)),
            dma((pairs,)),
            dma((pairs,)),
        ],
        compiler_params=pltpu.CompilerParams(
            collective_id=0, has_side_effects=True, vmem_limit_bytes=48 * 1024 * 1024
        ),
    )(spectra, masks)


def with_halo(cells, width):
    head = cells[..., :width]
    tail = cells[..., cells.shape[-1] - width:]
    return jnp.concatenate(
        [lax.ppermute(tail, "col", [(0, 1)]), cells, lax.ppermute(head, "col", [(1, 0)])], axis=-1
    )


def cosine_table(first, count):
    freqs = first + jnp.arange(count, dtype=jnp.int32)
    shifts = jnp.arange(1, LAGS + 1, dtype=jnp.int32)
    phase = freqs[:, None] * shifts[None, :] % (2 * F)
    angle = jnp.pi * phase.astype(jnp.float32) / F
    factor = 1.0 / math.sqrt(F)
    return jnp.concatenate([jnp.cos(angle) * factor, -jnp.sin(angle) * factor], axis=0).astype(jnp.bfloat16)


def correlate(own, own_live, far, far_live, table):
    a, b = own[:, 0].astype(jnp.float32), own[:, 1].astype(jnp.float32)
    c, d = far[:, 0].astype(jnp.float32), far[:, 1].astype(jnp.float32)
    shape = (own.shape[2], far.shape[2], own.shape[3])
    real = jnp.zeros(shape, jnp.float32)
    imag = jnp.zeros(shape, jnp.float32)
    for w in range(own.shape[0]):
        real = real + (a[w, :, None] * c[w, None] + b[w, :, None] * d[w, None])
        imag = imag + (b[w, :, None] * c[w, None] - a[w, :, None] * d[w, None])
    count = jnp.maximum(jnp.dot(own_live.T, far_live, preferred_element_type=jnp.float32), 1.0)
    stacked = (jnp.stack([real, imag], axis=2) / count[:, :, None, None]).astype(jnp.bfloat16)
    lines = stacked.reshape(shape[0] * shape[1], -1)
    return jnp.dot(lines, table, preferred_element_type=jnp.float32).reshape(shape[0], shape[1], LAGS)


def ring(spectra, masks):
    ch, half = spectra.shape[2], spectra.shape[3]
    rows = lax.axis_size("row")
    me, col = lax.axis_index("row"), lax.axis_index("col")
    quarter = ch // 2
    live = masks.astype(jnp.float32)
    values = spectra.astype(jnp.float32)
    padded = with_halo(jnp.sqrt(values[:, 0] * values[:, 0] + values[:, 1] * values[:, 1]), SMOOTH)
    total = padded
    for by in (1, 2, 4, 8, 16, 32):
        total = total[..., :-by] + total[..., by:]
    total = total[..., :half] + padded[..., 2 * SMOOTH:]
    amplitude = total / (2 * SMOOTH + 1) + EPSILON
    whitened = (values / amplitude[:, None] * live[:, None, :, None]).astype(jnp.bfloat16)
    table = cosine_table(col * half, half)
    onward = [(r, (r + 1) % rows) for r in range(rows)]

    def step(n, carry):
        result, far, marks = carry
        block = correlate(whitened, live, far, marks.astype(jnp.float32), table)
        block = block.reshape(ch, 2, quarter, LAGS)
        source = lax.rem(me + rows - n, rows)
        result = lax.dynamic_update_slice(result, block, (0, 0, source * quarter, 0))
        return result, lax.ppermute(far, "row", onward), lax.ppermute(marks, "row", onward)

    empty = jnp.zeros((ch, 2, rows * quarter, LAGS), jnp.float32)
    result, _, _ = lax.fori_loop(0, rows, step, (empty, whitened, live.astype(jnp.bfloat16)))
    mine = lax.dynamic_slice_in_dim(result, col, 1, 1)
    other = lax.dynamic_slice_in_dim(result, 1 - col, 1, 1)
    return mine + lax.ppermute(other, "col", [(0, 1), (1, 0)])


def per_device(spectra, masks):
    windows, _, ch, half = spectra.shape
    rows = lax.axis_size("row")
    bins = half // rows
    fits = rows in (2, 4, 6, 8) and ch == 8 and bins % (2 * LANES) == 0 and windows % GROUP_SPLIT == 0 and windows <= LANES
    return fused(spectra, masks) if fits else ring(spectra, masks)


def solution(mesh):
    return jax.shard_map(
        per_device,
        mesh=mesh,
        in_specs=(P("hours", None, "row", "col"), P("hours", "row")),
        out_specs=P(("hours", "row"), "col", None, None),
        check_vma=False,
    )
```
